32 devices in a mesh: groups: 2 (over y), pool: 8 (over z, x), tp: 2 (over core).
Axes of the slice: x: 2, y: 2, z: 4, core: 2. Of those that a mesh axis runs over, the one named last changes fastest.
Arguments:
- prompt_hidden: bfloat16 [8192, 256], P('pool', 'groups'), parts along dimension 1, may hold values from -6 to 6
- kv_weight: bfloat16 [2, 8192, 512], P(None, 'pool', 'tp'), may hold values from -0.0625 to 0.0625
- cache_kv: bfloat16 [2, 4096, 16, 512], P(None, ('groups', 'pool'), None, 'tp'), parts along dimension 1, may hold values from -6 to 6
- block_table: int32 [64, 64], P(('groups', 'pool')), parts along dimension 0, may hold values from 0 to 255, as said below
- cache_len: int32 [64], P(('groups', 'pool')), parts along dimension 0, may hold values from 1 to 1024, as said below
- page_request: int32 [16], P('groups'), parts along dimension 0, may hold values from 0 to 31, as said below
- prompt_len: int32 [64], P(('groups', 'pool')), parts along dimension 0, may hold values from 0 to 32, as said below
- query: bfloat16 [64, 4, 4096], P(('groups', 'pool'), None, 'tp'), parts along dimension 0, may hold values from -64 to 64
- new_kv: bfloat16 [2, 64, 4, 512], P(None, ('groups', 'pool'), None, 'tp'), parts along dimension 1, may hold values from -6 to 6
Outputs:
- attended: bfloat16 [64, 4, 4096], P(('groups', 'pool'), None, 'tp'), parts along dimension 0
The draws below stay inside these ranges and needn't reach their ends.
There are 2 independent parts, one for each index of `groups`. The reference program is written for one: setup_inputs(seed, part) draws one part's arguments, and reference() takes and returns one part's arrays. A program takes and returns all parts, laid end to end along the dimension named above; an argument that names none is the same for every part. Nothing has to cross between parts.
Inputs may be any that keep to these rules, and one draw needn't show every extreme that they name: `block_table`: row r holds 64 distinct pages of its owner's pool, local numbers; the rows of one owner together use each of its 256 pages once. `cache_len`: at least one request has the full 64 * 16 cached tokens. `page_request`: Non-decreasing; request 0 has exactly the first 2 pages, every other request at most one page, and request 32 - 1 has one. `prompt_len`: zero for requests without prompt pages; otherwise more than 16 times one less than their page count and at most 16 times it; request 0 has exactly 32.
All inputs are finite; a program needn't handle non-finite values.
Results may differ from the reference program's by a relative error of at most 0.0059.
Values may be sent and summed in bfloat16 or wider, within the bound.
No kernel may reach another device: no remote copies, remote signals or barrier semaphores. Data moves between devices by JAX's collectives and lax.ppermute only.
A program may use at most 64 MiB of HBM per device.

```python
import jax
import jax.numpy as jnp
from jax import lax

D = 8192
HEADS_Q = 32
HEADS_KV = 4
HEAD_DIM = 128
BLK = 16
STEPS = 4
REQ_DEV = 4
OLD_DEV = 256
MAXB = 64
REQS = 32
PPAGES = 8
PTOK = 128
KV_COLS = 512
Q_COLS = 4096
N_POOL = 8


def prompt_plan(key):
    key_order, key_extra = jax.random.split(key, 2)
    head_pages = PPAGES // 4
    rest_pages = PPAGES - head_pages
    order = jax.random.permutation(key_order, REQS - 1)[:rest_pages] + 1
    present = jnp.any(order == REQS - 1)
    order = jnp.where(present, order, order.at[0].set(REQS - 1))
    rest = jnp.sort(order)
    page_request = jnp.concatenate([jnp.zeros((head_pages,), jnp.int32), rest.astype(jnp.int32)]).astype(jnp.int32)
    request_ids = jnp.arange(REQS, dtype=jnp.int32)
    counts = jnp.sum((page_request[None, :] == request_ids[:, None]).astype(jnp.int32), axis=1)
    extra_tokens = jax.random.randint(key_extra, (REQS,), 1, BLK + 1)
    extra_tokens = extra_tokens.at[0].set(BLK)
    prompt_len = jnp.where(counts > 0, (counts - 1) * BLK + extra_tokens, 0).astype(jnp.int32)
    return (page_request, prompt_len)


def draw_page_request(key, part):
    shared = jax.random.fold_in(key, 7)
    return prompt_plan(shared)[0]


def draw_prompt_len(key, part):
    shared = jax.random.fold_in(key, 7)
    return prompt_plan(shared)[1]


def draw_block_table(key, part):
    key = jax.random.fold_in(key, 1)
    device_keys = jax.random.split(key, N_POOL)
    orders = jax.vmap(lambda single: jax.random.permutation(single, OLD_DEV))(device_keys)
    return orders.reshape(REQS, MAXB).astype(jnp.int32)


def draw_cache_len(key, part):
    key = jax.random.fold_in(key, 2)
    key_left, key_right = jax.random.split(key)
    longest = MAXB * BLK
    left_draw = jax.random.randint(key_left, (REQS,), 1, longest + 1)
    right_draw = jax.random.randint(key_right, (REQS,), 1, longest + 1)
    lengths = jnp.maximum(1, left_draw * right_draw // longest)
    return lengths.at[0].set(longest).astype(jnp.int32)


def draw_query(key, part):
    key = jax.random.fold_in(key, 11)
    key_base = jax.random.fold_in(key, 0)
    shape = (REQS, STEPS, Q_COLS)
    values = jnp.clip(jax.random.normal(key_base, shape, jnp.float32), -6.0, 6.0)
    return values.astype(jnp.bfloat16)


def strengthened(result, stream_key, source, target, blocks, factor):
    def block_of(axis_at):
        return (jnp.arange(result.shape[axis_at]) // (result.shape[axis_at] // blocks)).reshape((-1,) + (1,) * (result.ndim - 1 - axis_at))

    first = jax.random.permutation(stream_key, blocks)[block_of(target)]
    second = (block_of(target) + blocks // 2) % blocks
    return jnp.where((block_of(source) == first) | (block_of(source) == second), factor * result, result)


def level_of(rng, dims, pieces, least, high):
    def one(axis_at, shards_of):
        draws = jax.random.uniform(jax.random.fold_in(jax.random.fold_in(rng, 6), axis_at), (shards_of,), jnp.float32, least / len(pieces), high / len(pieces))
        return jnp.repeat(jnp.exp(draws), dims[axis_at] // shards_of).reshape((-1,) + (1,) * (len(dims) - axis_at - 1))

    level = one(*pieces[0])
    for cut in pieces[1:]:
        level = level * one(*cut)
    return level


def bell_draw(rng, dims, scale, bound, cuts=(), kind=jnp.bfloat16):
    level = level_of(rng, dims, cuts, -0.22, 0.18) if cuts else 1.0
    drawn = jax.random.normal(rng, dims, jnp.float32) * scale * level
    return jnp.minimum(jnp.maximum(drawn, -bound), bound).astype(kind)


def gaussian_with(key, dims, scale, most, cuts, heavy, kind=jnp.bfloat16):
    result = scale * jax.random.normal(key, dims, jnp.float32)
    if cuts:
        result = result * level_of(key, dims, cuts, -0.22, 0.18)
    return jnp.clip(strengthened(result, jax.random.fold_in(key, 3), *heavy), -most, most).astype(kind)


def setup_inputs(seed: int = 0, part: int = 0) -> dict:
    seeds = jax.random.split(jax.random.key(seed), 10)
    part_splits = jax.random.split(jax.random.fold_in(seeds[9], part), 10)
    return {
        "prompt_hidden": gaussian_with(part_splits[0], (D, PTOK), 1.0, 6.0, ((0, 8),), (0, 1, 8, 2.0)),
        "kv_weight": bell_draw(seeds[1], (2, D, KV_COLS), D ** -0.5, 0.0625, ((1, 8), (2, 2))),
        "cache_kv": bell_draw(part_splits[2], (2, REQS * MAXB, BLK, KV_COLS), 1.0, 6.0, ((1, 8), (3, 2))),
        "block_table": draw_block_table(jax.random.fold_in(jax.random.fold_in(seeds[9], part), 71), part),
        "cache_len": draw_cache_len(jax.random.fold_in(jax.random.fold_in(seeds[9], part), 71), part),
        "page_request": draw_page_request(jax.random.fold_in(jax.random.fold_in(seeds[9], part), 71), part),
        "prompt_len": draw_prompt_len(jax.random.fold_in(jax.random.fold_in(seeds[9], part), 71), part),
        "query": draw_query(jax.random.fold_in(jax.random.fold_in(seeds[9], part), 71), part),
        "new_kv": bell_draw(part_splits[8], (2, REQS, STEPS, KV_COLS), 1.0, 6.0, ((1, 8), (3, 2))),
    }


def reference(prompt_hidden, kv_weight, cache_kv, block_table, cache_len, page_request, prompt_len, query, new_kv):
    contract_dims = (((0,), (0,)), ((), ()))
    prompt_keys = lax.dot_general(prompt_hidden, kv_weight[0], contract_dims, preferred_element_type=jnp.float32).astype(jnp.bfloat16)
    prompt_values = lax.dot_general(prompt_hidden, kv_weight[1], contract_dims, preferred_element_type=jnp.float32).astype(jnp.bfloat16)
    per_group = HEADS_Q // HEADS_KV
    prompt_k32 = prompt_keys.astype(jnp.float32).reshape(PTOK, HEADS_KV, HEAD_DIM)
    prompt_v32 = prompt_values.astype(jnp.float32).reshape(PTOK, HEADS_KV, HEAD_DIM)
    token_index = jnp.arange(PTOK, dtype=jnp.int32)
    token_owner = jnp.repeat(page_request, BLK)
    request_ids = jnp.arange(REQS, dtype=jnp.int32)
    first_page = jnp.sum((page_request[None, :] < request_ids[:, None]).astype(jnp.int32), axis=1)
    score_scale = HEAD_DIM ** -0.5
    causal = jnp.arange(STEPS)[None, :] <= jnp.arange(STEPS)[:, None]

    def per_request(request):
        owner_dev = request // REQ_DEV
        page_ids = (owner_dev * OLD_DEV + block_table[request]).astype(jnp.int32)
        old_kv = cache_kv[:, page_ids].astype(jnp.float32).reshape(2, MAXB * BLK, HEADS_KV, HEAD_DIM)
        fresh_kv = new_kv[:, request].astype(jnp.float32).reshape(2, STEPS, HEADS_KV, HEAD_DIM)
        queries = query[request].astype(jnp.float32).reshape(STEPS, HEADS_KV, per_group, HEAD_DIM)
        score_old = jnp.einsum('sgqd,tgd->sgqt', queries, old_kv[0])
        score_prompt = jnp.einsum('sgqd,tgd->sgqt', queries, prompt_k32)
        score_new = jnp.einsum('sgqd,ugd->sgqu', queries, fresh_kv[0])
        old_mask = jnp.arange(MAXB * BLK) < cache_len[request]
        prompt_mask = (token_owner == request) & (token_index - BLK * first_page[request] < prompt_len[request])
        full_mask = jnp.concatenate([
            jnp.broadcast_to(old_mask[None, :], (STEPS, MAXB * BLK)),
            jnp.broadcast_to(prompt_mask[None, :], (STEPS, PTOK)),
            causal], axis=1)[:, None, None, :]
        scores = jnp.concatenate([score_old, score_prompt, score_new], axis=-1) * score_scale
        scores = jnp.where(full_mask, scores, -jnp.inf)
        row_max = jnp.max(scores, axis=-1, keepdims=True)
        shifted = jnp.exp(scores - row_max)
        weights = (shifted / jnp.sum(shifted, axis=-1, keepdims=True)).astype(jnp.bfloat16)
        weights = lax.optimization_barrier(weights).astype(jnp.float32)
        values = jnp.concatenate([old_kv[1], prompt_v32, fresh_kv[1]], axis=0)
        outputs = jnp.einsum('sgqt,tgd->sgqd', weights, values)
        return outputs.reshape(STEPS, Q_COLS).astype(jnp.bfloat16)

    return lax.map(per_request, request_ids)
```

```python
import functools
import math

import jax
import jax.numpy as jnp
from jax import lax
from jax.experimental import pallas as pl
from jax.experimental.pallas import tpu as pltpu
from jax.sharding import PartitionSpec as P

HEAD_DIM = 128
PER_GROUP = 8
SCALE = HEAD_DIM**-0.5 * math.log2(math.e)
LOW = -1e30

VMEM = pl.BlockSpec(memory_space=pltpu.VMEM)
SMEM = pl.BlockSpec(memory_space=pltpu.SMEM)
HBM = pl.BlockSpec(memory_space=pltpu.HBM)


def in_hbm(*arrays):
    return [pltpu.with_memory_space_constraint(x, pltpu.HBM) for x in arrays]


def dot_nt(a, b):
    return lax.dot_general(a, b, (((1,), (1,)), ((), ())), preferred_element_type=jnp.float32)


def pages_before(owner_ref, request):
    count = jnp.int32(0)
    for p in range(owner_ref.shape[0]):
        count = count + jnp.where(owner_ref[p] < request, 1, 0)
    return count


def window_sizes(page_total, reqs):
    least = page_total // 4
    return list(range(least, min(page_total, least + reqs - 1) + 1))


def project_kernel(
    pieces, reqs, page, partners, hidden_ref, weight_ref, owner_hbm, own_ref, *rest
):
    if partners:
        send_ref, plan_ref, hidden_buf, weight_buf, owner_ref, sems, owner_sem = rest
    else:
        hidden_buf, weight_buf, owner_ref, sems, owner_sem = rest
    cols = weight_ref.shape[2]
    size = hidden_ref.shape[0] // pieces
    copies = []
    for i in range(pieces):
        at = pl.ds(i * size, size)
        copies.append(
            (
                pltpu.make_async_copy(hidden_ref.at[at], hidden_buf.at[at], sems.at[0, i]),
                pltpu.make_async_copy(weight_ref.at[0, at], weight_buf.at[0, at], sems.at[1, i]),
                pltpu.make_async_copy(weight_ref.at[1, at], weight_buf.at[1, at], sems.at[2, i]),
            )
        )
    owner_copy = pltpu.make_async_copy(owner_hbm, owner_ref, owner_sem)
    owner_copy.start()
    for group in copies:
        for copy in group:
            copy.start()
    owner_copy.wait()
    me = lax.axis_index("pool")
    for i, partner in enumerate(partners):
        first = pages_before(owner_ref, (me ^ partner) * reqs)
        plan_ref[i] = jnp.full(plan_ref.shape[1:], first, jnp.int32)
    totals = [0.0, 0.0]
    for i in range(pieces):
        for copy in copies[i]:
            copy.wait()
        at = slice(i * size, (i + 1) * size)
        for kind in range(2):
            totals[kind] = totals[kind] + lax.dot_general(
                hidden_buf[at],
                weight_buf[kind, at],
                (((0,), (0,)), ((), ())),
                preferred_element_type=jnp.float32,
            )
    for kind in range(2):
        own_ref[:, kind * cols : (kind + 1) * cols] = totals[kind].astype(jnp.bfloat16)
    if partners:
        begin = pl.multiple_of((1 - (me & 1)) * page, page)
        send_ref[...] = own_ref[pl.ds(begin, send_ref.shape[0]), :]


def project(hidden, weight, owner, reqs, page, partners):
    tokens, cols = hidden.shape[1], weight.shape[2]
    pieces = max(1, hidden.shape[0] // 256)
    out_shape = [jax.ShapeDtypeStruct((tokens, 2 * cols), jnp.bfloat16)]
    if partners:
        out_shape += [
            jax.ShapeDtypeStruct((tokens - page, 2 * cols), jnp.bfloat16),
            jax.ShapeDtypeStruct((len(partners), 8, HEAD_DIM), jnp.int32),
        ]
    return pl.pallas_call(
        functools.partial(project_kernel, pieces, reqs, page, partners),
        out_shape=out_shape,
        in_specs=[HBM] * 3,
        out_specs=[VMEM] * len(out_shape),
        scratch_shapes=[
            pltpu.VMEM(hidden.shape, jnp.bfloat16),
            pltpu.VMEM(weight.shape, jnp.bfloat16),
            pltpu.SMEM(owner.shape, jnp.int32),
            pltpu.SemaphoreType.DMA((3, pieces)),
            pltpu.SemaphoreType.DMA,
        ],
        compiler_params=pltpu.CompilerParams(vmem_limit_bytes=24 * 2**20),
        cost_estimate=pl.CostEstimate(
            flops=4 * hidden.size * cols,
            bytes_accessed=2 * (hidden.size + weight.size + tokens * 2 * cols),
            transcendentals=0,
        ),
        name="project",
    )(*in_hbm(hidden, weight, owner))


def pick_kernel(page, own_ref, got_ref, plan_ref, *rest):
    outs, total_ref = rest[:-1], rest[-1]
    tokens = own_ref.shape[0]
    begin = pl.multiple_of((lax.axis_index("pool") & 1) * page, page)
    at = pl.ds(begin, got_ref.shape[0])
    total_ref[...] = own_ref[...]
    total_ref[at, :] = (own_ref[at, :].astype(jnp.float32) + got_ref[...].astype(jnp.float32)).astype(
        jnp.bfloat16
    )
    total = total_ref[...]
    for i, out in enumerate(outs):
        rows = out.shape[0]
        shape = (rows // 8, 8, tokens)
        row = lax.broadcasted_iota(jnp.int32, shape, 0) * 8 + lax.broadcasted_iota(jnp.int32, shape, 1)
        col = lax.broadcasted_iota(jnp.int32, shape, 2)
        begin = jnp.minimum(plan_ref[i], (tokens - rows) // page)[None, :, :1] * page
        take = jnp.where(col - row == begin, 1.0, 0.0).reshape(rows, tokens).astype(jnp.bfloat16)
        out[...] = jnp.dot(take, total, preferred_element_type=jnp.float32).astype(jnp.bfloat16)


def pick(own, got, plan, rows, page):
    shape = jax.ShapeDtypeStruct((rows, own.shape[1]), jnp.bfloat16)
    count = plan.shape[0]
    return pl.pallas_call(
        functools.partial(pick_kernel, page),
        out_shape=[shape] * count,
        in_specs=[VMEM] * 3,
        out_specs=[VMEM] * count,
        scratch_shapes=[pltpu.VMEM(own.shape, jnp.bfloat16)],
        compiler_params=pltpu.CompilerParams(vmem_limit_bytes=24 * 2**20),
        cost_estimate=pl.CostEstimate(
            flops=2 * count * rows * own.size, bytes_accessed=4 * own.size, transcendentals=0
        ),
        name="pick",
    )(own, got, plan)


def cached_kernel(
    reqs, steps, groups, pages, owners,
    table_hbm, len_hbm, owner_hbm, prompt_hbm, cache_ref, query_hbm, new_hbm,
    q_out, o_out, m_out, l_out, bias_out, size_out,
    table_ref, len_ref, owner_ref, prompt_ref, query_ref, new_ref, kbuf, vbuf, qf, newf, sems, small,
):
    page = kbuf.shape[1]
    span = pages * page
    rows = groups * steps * PER_GROUP
    pieces = sems.shape[1]
    size = kbuf.shape[0] // pieces
    first_loads = [
        pltpu.make_async_copy(src, dst, small.at[i])
        for i, (src, dst) in enumerate(
            (
                (query_hbm, query_ref),
                (new_hbm, new_ref),
                (table_hbm, table_ref),
                (len_hbm, len_ref),
                (owner_hbm, owner_ref),
                (prompt_hbm, prompt_ref),
            )
        )
    ]
    copies = [
        [
            pltpu.make_async_copy(
                cache_ref.at[kind, pl.ds(i * size, size)],
                buf.at[pl.ds(i * size, size)],
                sems.at[kind, i],
            )
            for i in range(pieces)
        ]
        for kind, buf in enumerate((kbuf, vbuf))
    ]
    for copy in first_loads + copies[0] + copies[1]:
        copy.start()
    for copy in first_loads:
        copy.wait()

    me = lax.axis_index("pool")
    page_total = owner_ref.shape[0]
    begin = jnp.int32(0)
    if owners:
        least = window_sizes(page_total, reqs)[0]
        edges = [pages_before(owner_ref, o * reqs) for o in range(owners)] + [jnp.int32(page_total)]
        most = jnp.int32(least)
        for low, high in zip(edges, edges[1:]):
            most = jnp.maximum(most, high - low)
        size_out[0] = most - least
        begin = jnp.minimum(pages_before(owner_ref, me * reqs), page_total - most) * page
    else:
        size_out[0] = jnp.int32(0)
    col = lax.broadcasted_iota(jnp.int32, bias_out.shape[1:], 1) + begin
    for r in range(reqs):
        first = pages_before(owner_ref, me * reqs + r)
        last = pages_before(owner_ref, me * reqs + r + 1)
        end = jnp.minimum(first * page + prompt_ref[r], last * page)
        bias_out[r] = jnp.where((col >= first * page) & (col < end), 0.0, LOW)

    for r in range(reqs):
        for g in range(groups):
            for h in range(PER_GROUP):
                at = (g * PER_GROUP + h) * HEAD_DIM
                qf[pl.ds(r * rows + g * steps * PER_GROUP + h, steps, stride=PER_GROUP), :] = query_ref[
                    r, :, at : at + HEAD_DIM
                ].astype(jnp.float32)
    q_all = qf[...]
    row = lax.broadcasted_iota(jnp.int32, q_all.shape, 0)
    row_group = (row // (steps * PER_GROUP)) % groups
    q_out[...] = jnp.concatenate(
        [jnp.where(row_group == g, q_all, 0.0).astype(jnp.bfloat16) for g in range(groups)], axis=1
    )

    slot = HEAD_DIM // reqs
    newf[...] = jnp.zeros_like(newf)
    for kind in range(2):
        for r in range(reqs):
            newf[kind, r * slot : r * slot + steps, :] = new_ref[kind, r].astype(jnp.float32)
    new_k = newf[0].astype(jnp.bfloat16)
    new_v = newf[1].astype(jnp.bfloat16)

    for copy in copies[0]:
        copy.wait()
    scores, news, maxes = [], [], []
    for r in range(reqs):
        q = q_out[r * rows : (r + 1) * rows, :]
        s_new = dot_nt(q, new_k) * SCALE
        row = lax.broadcasted_iota(jnp.int32, s_new.shape, 0)
        col = lax.broadcasted_iota(jnp.int32, s_new.shape, 1) - r * slot
        step = (row // PER_GROUP) % steps
        s_new = jnp.where((col >= 0) & (col <= step), s_new, LOW)
        news.append(s_new)
        k = jnp.concatenate([kbuf[table_ref[r, j]] for j in range(pages)], axis=0)
        s = dot_nt(q, k) * SCALE
        col = lax.broadcasted_iota(jnp.int32, s.shape, 1)
        s = jnp.where(col < len_ref[r], s, LOW)
        scores.append(s)
        top = s_new
        for c in range(span // HEAD_DIM):
            top = jnp.maximum(top, s[:, c * HEAD_DIM : (c + 1) * HEAD_DIM])
        m = jnp.max(top, axis=1, keepdims=True)
        maxes.append(m)
        m_out[r * rows : (r + 1) * rows, :] = jnp.broadcast_to(m, (rows, HEAD_DIM))
    for copy in copies[1]:
        copy.wait()
    for r in range(reqs):
        p = jnp.exp2(scores[r] - maxes[r])
        p_new = jnp.exp2(news[r] - maxes[r])
        total = p_new
        for c in range(span // HEAD_DIM):
            total = total + p[:, c * HEAD_DIM : (c + 1) * HEAD_DIM]
        l_out[r * rows : (r + 1) * rows, :] = jnp.broadcast_to(
            jnp.sum(total, axis=1, keepdims=True), (rows, HEAD_DIM)
        )
        v = jnp.concatenate([vbuf[table_ref[r, j]] for j in range(pages)], axis=0)
        o = jnp.dot(p.astype(jnp.bfloat16), v, preferred_element_type=jnp.float32)
        o = o + jnp.dot(p_new.astype(jnp.bfloat16), new_v, preferred_element_type=jnp.float32)
        part = rows // groups
        for g in range(groups):
            o_out[r * rows + g * part : r * rows + (g + 1) * part, :] = o[
                g * part : (g + 1) * part, g * HEAD_DIM : (g + 1) * HEAD_DIM
            ]


def cached(table, length, owner, prompt_len, cache, query, new, tokens, owners):
    reqs, steps = query.shape[:2]
    groups = cache.shape[3] // HEAD_DIM
    pages, page = table.shape[1], cache.shape[2]
    rows = reqs * groups * steps * PER_GROUP
    flat = jax.ShapeDtypeStruct((rows, HEAD_DIM), jnp.float32)
    return pl.pallas_call(
        functools.partial(cached_kernel, reqs, steps, groups, pages, owners),
        out_shape=[
            jax.ShapeDtypeStruct((rows, groups * HEAD_DIM), jnp.bfloat16),
            flat,
            flat,
            flat,
            jax.ShapeDtypeStruct((reqs, 8, tokens), jnp.float32),
            jax.ShapeDtypeStruct((1,), jnp.int32),
        ],
        in_specs=[HBM] * 7,
        out_specs=[VMEM] * 5 + [SMEM],
        scratch_shapes=[
            pltpu.SMEM(table.shape, jnp.int32),
            pltpu.SMEM(length.shape, jnp.int32),
            pltpu.SMEM(owner.shape, jnp.int32),
            pltpu.SMEM(prompt_len.shape, jnp.int32),
            pltpu.VMEM(query.shape, jnp.bfloat16),
            pltpu.VMEM(new.shape, jnp.bfloat16),
            pltpu.VMEM(cache.shape[1:], jnp.bfloat16),
            pltpu.VMEM(cache.shape[1:], jnp.bfloat16),
            pltpu.VMEM((rows, HEAD_DIM), jnp.float32),
            pltpu.VMEM((2, HEAD_DIM, groups * HEAD_DIM), jnp.float32),
            pltpu.SemaphoreType.DMA((2, 4)),
            pltpu.SemaphoreType.DMA((6,)),
        ],
        compiler_params=pltpu.CompilerParams(vmem_limit_bytes=32 * 2**20),
        cost_estimate=pl.CostEstimate(
            flops=8 * rows * pages * page * HEAD_DIM,
            bytes_accessed=2 * cache.size,
            transcendentals=rows * pages * page,
        ),
        name="cached",
    )(*in_hbm(table, length, owner, prompt_len, cache, query, new))


def prompt_kernel(reqs, steps, groups, count, *refs):
    parts = refs[:count]
    q_ref, o_ref, m_ref, l_ref, bias_ref, out_ref, of = refs[count:]
    width = groups * HEAD_DIM
    rows = groups * steps * PER_GROUP
    tokens = bias_ref.shape[2]
    rows_kv = parts[0][...]
    if count > 1:
        total = rows_kv.astype(jnp.float32)
        for part in parts[1:]:
            total = total + part[...].astype(jnp.float32)
        rows_kv = total.astype(jnp.bfloat16)
    if rows_kv.shape[0] < tokens:
        rows_kv = jnp.concatenate(
            [rows_kv, jnp.zeros((tokens - rows_kv.shape[0], 2 * width), jnp.bfloat16)], axis=0
        )
    k, v = rows_kv[:, :width], rows_kv[:, width:]
    s_all = dot_nt(q_ref[...], k) * SCALE
    for r in range(reqs):
        at = slice(r * rows, (r + 1) * rows)
        s = (s_all[at].reshape(rows // 8, 8, tokens) + bias_ref[r][None]).reshape(rows, tokens)
        m_old = m_ref[at]
        m = jnp.maximum(m_old, jnp.max(s, axis=1, keepdims=True))
        alpha = jnp.exp2(m_old - m)
        p_new = jnp.exp2(s - m[:, :1])
        l = l_ref[at] * alpha + jnp.sum(p_new, axis=1, keepdims=True)
        pv = jnp.dot(p_new.astype(jnp.bfloat16), v, preferred_element_type=jnp.float32)
        part = rows // groups
        pv = jnp.concatenate(
            [pv[g * part : (g + 1) * part, g * HEAD_DIM : (g + 1) * HEAD_DIM] for g in range(groups)],
            axis=0,
        )
        of[at] = (o_ref[at] * alpha + pv) / l
    for r in range(reqs):
        for g in range(groups):
            for h in range(PER_GROUP):
                at = (g * PER_GROUP + h) * HEAD_DIM
                out_ref[r, :, at : at + HEAD_DIM] = of[
                    pl.ds(r * rows + g * steps * PER_GROUP + h, steps, stride=PER_GROUP), :
                ].astype(jnp.bfloat16)


def prompt(state, parts, query):
    reqs, steps = query.shape[:2]
    groups = parts[0].shape[1] // (2 * HEAD_DIM)
    q, o, m, l, bias = state
    return pl.pallas_call(
        functools.partial(prompt_kernel, reqs, steps, groups, len(parts)),
        out_shape=jax.ShapeDtypeStruct(query.shape, jnp.bfloat16),
        in_specs=[VMEM] * (5 + len(parts)),
        out_specs=VMEM,
        scratch_shapes=[pltpu.VMEM(o.shape, jnp.float32)],
        compiler_params=pltpu.CompilerParams(vmem_limit_bytes=24 * 2**20),
        name="prompt",
    )(*parts, q, o, m, l, bias)


def add_kernel(parts_ref, out_ref):
    total = parts_ref[0].astype(jnp.float32)
    for k in range(1, parts_ref.shape[0]):
        total = total + parts_ref[k].astype(jnp.float32)
    out_ref[...] = total.astype(jnp.bfloat16)


def add(parts):
    return pl.pallas_call(
        add_kernel,
        out_shape=jax.ShapeDtypeStruct(parts.shape[1:], jnp.bfloat16),
        in_specs=[VMEM],
        out_specs=VMEM,
        compiler_params=pltpu.CompilerParams(vmem_limit_bytes=24 * 2**20),
        name="add",
    )(parts)


def on_device(
    pool, prompt_hidden, kv_weight, cache_kv, block_table, cache_len, page_request, prompt_len, query, new_kv
):
    reqs, page, pages = query.shape[0], cache_kv.shape[2], page_request.shape[0]
    tokens = pages * page
    inputs = (block_table, cache_len, page_request, prompt_len, cache_kv, query, new_kv)
    if pool in (4, 8):
        partners = [0] + [p for p in (4, 6, 2) if p < pool]
        sizes = window_sizes(pages, reqs)
        own, send, plan = project(prompt_hidden, kv_weight, page_request, reqs, page, partners)
        got = lax.ppermute(send, "pool", [(i, i ^ 1) for i in range(pool)])
        *state, size = cached(*inputs, -(-sizes[-1] * page // HEAD_DIM) * HEAD_DIM, pool)

        def share(window, own, got, plan, state):
            cuts = pick(own, got, plan, window * page, page)
            parts = [cuts[0]] + [
                lax.ppermute(cut, "pool", [(i, i ^ p) for i in range(pool)])
                for cut, p in zip(cuts[1:], partners[1:])
            ]
            return prompt(state, parts, query)

        branches = [functools.partial(share, window) for window in sizes]
        return lax.switch(size[0], branches, own, got, plan, state)
    [own] = project(prompt_hidden, kv_weight, page_request, reqs, page, [])
    got = lax.all_to_all(own.reshape(pool, tokens // pool, -1), "pool", 0, 0, tiled=True)
    mine = add(got)
    shared = lax.all_to_all(jnp.broadcast_to(mine, got.shape), "pool", 0, 0, tiled=True)
    *state, _ = cached(*inputs, tokens, 0)
    return prompt(state, [shared.reshape(tokens, -1)], query)


def solution(mesh):
    in_specs = (
        P("pool", "groups"),
        P(None, "pool", "tp"),
        P(None, ("groups", "pool"), None, "tp"),
        P(("groups", "pool"), None),
        P(("groups", "pool")),
        P("groups"),
        P(("groups", "pool")),
        P(("groups", "pool"), None, "tp"),
        P(None, ("groups", "pool"), None, "tp"),
    )
    out_specs = P(("groups", "pool"), None, "tp")
    return jax.shard_map(
        functools.partial(on_device, mesh.shape["pool"]),
        mesh=mesh,
        in_specs=in_specs,
        out_specs=out_specs,
        check_vma=False,
    )
```

```python
import functools
import math

import jax
import jax.numpy as jnp
from jax import lax
from jax.experimental import pallas as pl
from jax.experimental.pallas import tpu as pltpu
from jax.sharding import PartitionSpec as P

HEAD_DIM = 128
PER_GROUP = 8
SCALE = HEAD_DIM**-0.5 * math.log2(math.e)
LOW = -1e30

VMEM = pl.BlockSpec(memory_space=pltpu.VMEM)
SMEM = pl.BlockSpec(memory_space=pltpu.SMEM)
HBM = pl.BlockSpec(memory_space=pltpu.HBM)
ANY = pl.BlockSpec(memory_space=pl.ANY)


def in_hbm(*arrays):
    return [pltpu.with_memory_space_constraint(x, pltpu.HBM) for x in arrays]


def dot_nt(a, b):
    return lax.dot_general(a, b, (((1,), (1,)), ((), ())), preferred_element_type=jnp.float32)


def pages_before(owner_ref, request):
    count = jnp.int32(0)
    for p in range(owner_ref.shape[0]):
        count = count + jnp.where(owner_ref[p] < request, 1, 0)
    return count


def step_sizes(page_total, reqs):
    most = (page_total - 1, min(page_total, page_total // 4 + reqs - 1))
    usual = [(3, 2), (3, 3), (4, 3), (4, 4)]
    return [u for u in usual if u[0] < most[0] and u[1] <= most[1]] + [most]


def plan_steps(owner_ref, reqs, page, sizes, choice_ref, lists, plan_refs):
    me = lax.axis_index("pool")
    page_total = owner_ref.shape[0]
    for ref in lists:
        for p in range(page_total):
            ref[p] = jnp.int32(0)
    filled = [jnp.int32(0)] * 6
    counts = [jnp.int32(0)] * 2
    for p in range(page_total):
        owner = lax.div(owner_ref[p], jnp.int32(reqs))
        counts[0] = counts[0] + lax.shift_left(jnp.int32(1), 4 * (owner & 3))
        counts[1] = counts[1] + lax.shift_left(jnp.int32(1), 4 * owner)
        away = owner ^ me
        place = filled[0]
        for i in range(6):
            if i < 4:
                here, value = (away & 3) == i, jnp.int32(p)
            else:
                here, value = away == 4 * (5 - i), place
            lists[i][jnp.where(here, filled[i], page_total)] = value
            filled[i] = filled[i] + jnp.where(here, 1, 0)
    most = []
    for count, classes in zip(counts, (4, 8)):
        top = jnp.int32(0)
        for c in range(classes):
            top = jnp.maximum(top, lax.shift_right_logical(count, jnp.int32(4 * c)) & 15)
        most.append(top)
    choice = jnp.int32(len(sizes) - 1)
    for i in reversed(range(len(sizes) - 1)):
        fits = (most[0] <= sizes[i][0]) & (most[1] <= sizes[i][1])
        choice = jnp.where(fits, i, choice)
    choice_ref[0] = choice
    row = lax.broadcasted_iota(jnp.int32, (page, HEAD_DIM), 0)
    for ref, plan in zip(lists[4:], plan_refs):
        for j in range(plan.shape[0] // page):
            plan[j * page : (j + 1) * page, :] = ref[j] * page + row


def project_kernel(pieces, reqs, page, sizes, hidden_ref, weight_ref, owner_hbm, *rest):
    if sizes:
        count = 3 * len({size[0] for size in sizes})
        sends, (keep_ref, *plan_refs, choice_ref) = rest[:count], rest[count : count + 4]
        own_ref, hidden_buf, turned_buf, weight_buf, owner_ref, sems, small, *lists = rest[count + 4 :]
    else:
        own_ref, hidden_buf, turned_buf, weight_buf, owner_ref, sems, small = rest
    cols = weight_ref.shape[2]
    size = hidden_ref.shape[0] // pieces
    hidden_copy = pltpu.make_async_copy(hidden_ref, hidden_buf, small.at[0])
    owner_copy = pltpu.make_async_copy(owner_hbm, owner_ref, small.at[1])
    copies = []
    for i in range(pieces):
        at = pl.ds(i * size, size)
        copies.append(
            pltpu.make_async_copy(weight_ref.at[:, at], weight_buf.at[:, at], sems.at[i])
        )
    for copy in [hidden_copy, owner_copy] + copies:
        copy.start()
    owner_copy.wait()
    if sizes:
        plan_steps(owner_ref, reqs, page, sizes, choice_ref, lists, plan_refs)
    hidden_copy.wait()
    turned_buf[...] = hidden_buf[...].T
    totals = [0.0, 0.0]
    for i in range(pieces):
        copies[i].wait()
        at = slice(i * size, (i + 1) * size)
        for kind in range(2):
            totals[kind] = totals[kind] + jnp.dot(
                turned_buf[:, at], weight_buf[kind, at], preferred_element_type=jnp.float32
            )
    for kind in range(2):
        own_ref[:, kind * cols : (kind + 1) * cols] = totals[kind].astype(jnp.bfloat16)
    if sizes:

        def pack(largest, chosen):
            for j in range(largest):
                at = slice(j * page, (j + 1) * page)
                cuts = [
                    own_ref[pl.ds(pl.multiple_of(lists[i][j] * page, page), page), :]
                    for i in range(4)
                ]
                keep_ref[at, :] = cuts[0]
                for i, send in chosen:
                    if send.shape[0] > j * page:
                        send[at, :] = cuts[1 + i % 3]

        last = len(sizes) - 1
        all_sends = list(enumerate(sends))
        if last:
            pl.when(choice_ref[0] < last)(lambda: pack(max(u[0] for u in sizes[:last]), all_sends[:-3]))
        pl.when(choice_ref[0] == last)(lambda: pack(sizes[last][0], all_sends[-3:]))


def project(hidden, weight, owner, reqs, page, sizes):
    tokens, cols = hidden.shape[1], weight.shape[2]
    pieces = max(1, hidden.shape[0] // 128)
    rows = lambda n: jax.ShapeDtypeStruct((n * page, 2 * cols), jnp.bfloat16)
    scratch = [
        pltpu.VMEM(hidden.shape, jnp.bfloat16),
        pltpu.VMEM(hidden.shape[::-1], jnp.bfloat16),
        pltpu.VMEM(weight.shape, jnp.bfloat16),
        pltpu.SMEM(owner.shape, jnp.int32),
        pltpu.SemaphoreType.DMA((pieces,)),
        pltpu.SemaphoreType.DMA((2,)),
    ]
    if sizes:
        first, second = sizes[-1]
        plan = jax.ShapeDtypeStruct((second * page, HEAD_DIM), jnp.int32)
        out_shape = [rows(n) for n in sorted({size[0] for size in sizes}) for _ in range(3)]
        out_shape += [rows(first), plan, plan]
        out_specs = [VMEM] * len(out_shape) + [SMEM]
        out_shape += [pltpu.SMEM((1,), jnp.int32)]
        scratch = [pltpu.VMEM((tokens, 2 * cols), jnp.bfloat16)] + scratch
        scratch += [pltpu.SMEM((owner.shape[0] + 1,), jnp.int32)] * 6
    else:
        out_shape, out_specs = [rows(tokens // page)], [VMEM]
    return pl.pallas_call(
        functools.partial(project_kernel, pieces, reqs, page, sizes),
        out_shape=out_shape,
        in_specs=[HBM] * 3,
        out_specs=out_specs,
        scratch_shapes=scratch,
        compiler_params=pltpu.CompilerParams(vmem_limit_bytes=24 * 2**20),
        cost_estimate=pl.CostEstimate(
            flops=4 * hidden.size * cols,
            bytes_accessed=2 * (hidden.size + weight.size + tokens * 2 * cols),
            transcendentals=0,
        ),
        name="project",
    )(*in_hbm(hidden, weight, owner))


def fold_kernel(keep_ref, *refs):
    got, (send_plan, keep_plan, _, send_out, keep_out) = refs[:-5], refs[-5:]
    rows = got[0].shape[0]
    total = keep_ref[:rows].astype(jnp.float32)
    for ref in got:
        total = total + ref[...].astype(jnp.float32)
    pad = jnp.zeros((HEAD_DIM - rows, total.shape[1]), jnp.bfloat16)
    total = jnp.concatenate([total.astype(jnp.bfloat16), pad], axis=0)
    for plan, out in ((send_plan, send_out), (keep_plan, keep_out)):
        at = plan[: out.shape[0]]
        col = lax.broadcasted_iota(jnp.int32, at.shape, 1)
        take = jnp.where(at == col, 1.0, 0.0).astype(jnp.bfloat16)
        out[...] = jnp.dot(take, total, preferred_element_type=jnp.float32).astype(jnp.bfloat16)


def fold(keep, got, plans, rows, after):
    out = jax.ShapeDtypeStruct((rows, keep.shape[1]), jnp.bfloat16)
    return pl.pallas_call(
        fold_kernel,
        out_shape=[out, out],
        in_specs=[VMEM] * (3 + len(got)) + [ANY],
        out_specs=[VMEM] * 2,
        compiler_params=pltpu.CompilerParams(vmem_limit_bytes=24 * 2**20),
        cost_estimate=pl.CostEstimate(
            flops=4 * rows * keep.size, bytes_accessed=8 * keep.size, transcendentals=0
        ),
        name="fold",
    )(keep, *got, *plans, after)


def cached_kernel(
    reqs, steps, groups, pages, packed,
    table_hbm, len_hbm, owner_hbm, prompt_hbm, cache_ref, query_hbm, new_hbm, after_ref,
    q_out, o_out, m_out, l_out, bias_out,
    table_ref, len_ref, owner_ref, prompt_ref, query_ref, new_ref, kbuf, vbuf, qf, newf, sems, small,
):
    page = kbuf.shape[1]
    span = pages * page
    rows = groups * steps * PER_GROUP
    pieces = sems.shape[1]
    size = kbuf.shape[0] // pieces
    first_loads = [
        pltpu.make_async_copy(src, dst, small.at[i])
        for i, (src, dst) in enumerate(
            (
                (query_hbm, query_ref),
                (new_hbm, new_ref),
                (table_hbm, table_ref),
                (len_hbm, len_ref),
                (owner_hbm, owner_ref),
                (prompt_hbm, prompt_ref),
            )
        )
    ]
    copies = [
        [
            pltpu.make_async_copy(
                cache_ref.at[kind, pl.ds(i * size, size)],
                buf.at[pl.ds(i * size, size)],
                sems.at[kind, i],
            )
            for i in range(pieces)
        ]
        for kind, buf in enumerate((kbuf, vbuf))
    ]
    for copy in first_loads + copies[0] + copies[1]:
        copy.start()
    for copy in first_loads:
        copy.wait()

    me = lax.axis_index("pool")
    firsts = [pages_before(owner_ref, me * reqs + r) for r in range(reqs + 1)]
    begin = firsts[0] * page if packed else 0
    col = lax.broadcasted_iota(jnp.int32, bias_out.shape[1:], 1) + begin
    for r, (first, last) in enumerate(zip(firsts, firsts[1:])):
        end = jnp.minimum(first * page + prompt_ref[r], last * page)
        bias_out[r] = jnp.where((col >= first * page) & (col < end), 0.0, LOW)

    for r in range(reqs):
        for g in range(groups):
            for h in range(PER_GROUP):
                at = (g * PER_GROUP + h) * HEAD_DIM
                qf[pl.ds(r * rows + g * steps * PER_GROUP + h, steps, stride=PER_GROUP), :] = query_ref[
                    r, :, at : at + HEAD_DIM
                ].astype(jnp.float32)
    q_all = qf[...]
    row = lax.broadcasted_iota(jnp.int32, q_all.shape, 0)
    row_group = (row // (steps * PER_GROUP)) % groups
    q_out[...] = jnp.concatenate(
        [jnp.where(row_group == g, q_all, 0.0).astype(jnp.bfloat16) for g in range(groups)], axis=1
    )

    slot = HEAD_DIM // reqs
    newf[...] = jnp.zeros_like(newf)
    for kind in range(2):
        for r in range(reqs):
            newf[kind, r * slot : r * slot + steps, :] = new_ref[kind, r].astype(jnp.float32)
    new_k = newf[0].astype(jnp.bfloat16)
    new_v = newf[1].astype(jnp.bfloat16)

    for copy in copies[0]:
        copy.wait()
    scores, news, maxes = [], [], []
    for r in range(reqs):
        q = q_out[r * rows : (r + 1) * rows, :]
        s_new = dot_nt(q, new_k) * SCALE
        row = lax.broadcasted_iota(jnp.int32, s_new.shape, 0)
        col = lax.broadcasted_iota(jnp.int32, s_new.shape, 1) - r * slot
        step = (row // PER_GROUP) % steps
        s_new = jnp.where((col >= 0) & (col <= step), s_new, LOW)
        news.append(s_new)
        k = jnp.concatenate([kbuf[table_ref[r, j]] for j in range(pages)], axis=0)
        s = dot_nt(q, k) * SCALE
        col = lax.broadcasted_iota(jnp.int32, s.shape, 1)
        s = jnp.where(col < len_ref[r], s, LOW)
        scores.append(s)
        top = s_new
        for c in range(span // HEAD_DIM):
            top = jnp.maximum(top, s[:, c * HEAD_DIM : (c + 1) * HEAD_DIM])
        m = jnp.max(top, axis=1, keepdims=True)
        maxes.append(m)
        m_out[r * rows : (r + 1) * rows, :] = jnp.broadcast_to(m, (rows, HEAD_DIM))
    for copy in copies[1]:
        copy.wait()
    for r in range(reqs):
        p = jnp.exp2(scores[r] - maxes[r])
        p_new = jnp.exp2(news[r] - maxes[r])
        total = p_new
        for c in range(span // HEAD_DIM):
            total = total + p[:, c * HEAD_DIM : (c + 1) * HEAD_DIM]
        l_out[r * rows : (r + 1) * rows, :] = jnp.broadcast_to(
            jnp.sum(total, axis=1, keepdims=True), (rows, HEAD_DIM)
        )
        v = jnp.concatenate([vbuf[table_ref[r, j]] for j in range(pages)], axis=0)
        o = jnp.dot(p.astype(jnp.bfloat16), v, preferred_element_type=jnp.float32)
        o = o + jnp.dot(p_new.astype(jnp.bfloat16), new_v, preferred_element_type=jnp.float32)
        part = rows // groups
        for g in range(groups):
            o_out[r * rows + g * part : r * rows + (g + 1) * part, :] = o[
                g * part : (g + 1) * part, g * HEAD_DIM : (g + 1) * HEAD_DIM
            ]


def cached(table, length, owner, prompt_len, cache, query, new, tokens, packed, after):
    reqs, steps = query.shape[:2]
    groups = cache.shape[3] // HEAD_DIM
    pages, page = table.shape[1], cache.shape[2]
    rows = reqs * groups * steps * PER_GROUP
    flat = jax.ShapeDtypeStruct((rows, HEAD_DIM), jnp.float32)
    return pl.pallas_call(
        functools.partial(cached_kernel, reqs, steps, groups, pages, packed),
        out_shape=[
            jax.ShapeDtypeStruct((rows, groups * HEAD_DIM), jnp.bfloat16),
            flat,
            flat,
            flat,
            jax.ShapeDtypeStruct((reqs, 8, tokens), jnp.float32),
        ],
        in_specs=[HBM] * 7 + [ANY],
        out_specs=[VMEM] * 5,
        scratch_shapes=[
            pltpu.SMEM(table.shape, jnp.int32),
            pltpu.SMEM(length.shape, jnp.int32),
            pltpu.SMEM(owner.shape, jnp.int32),
            pltpu.SMEM(prompt_len.shape, jnp.int32),
            pltpu.VMEM(query.shape, jnp.bfloat16),
            pltpu.VMEM(new.shape, jnp.bfloat16),
            pltpu.VMEM(cache.shape[1:], jnp.bfloat16),
            pltpu.VMEM(cache.shape[1:], jnp.bfloat16),
            pltpu.VMEM((rows, HEAD_DIM), jnp.float32),
            pltpu.VMEM((2, HEAD_DIM, groups * HEAD_DIM), jnp.float32),
            pltpu.SemaphoreType.DMA((2, 4)),
            pltpu.SemaphoreType.DMA((6,)),
        ],
        compiler_params=pltpu.CompilerParams(vmem_limit_bytes=32 * 2**20),
        cost_estimate=pl.CostEstimate(
            flops=8 * rows * pages * page * HEAD_DIM,
            bytes_accessed=2 * cache.size,
            transcendentals=rows * pages * page,
        ),
        name="cached",
    )(*in_hbm(table, length, owner, prompt_len, cache, query, new), after)


def prompt_kernel(reqs, steps, groups, count, *refs):
    parts = refs[:count]
    q_ref, o_ref, m_ref, l_ref, bias_ref, out_hbm, out_ref, of, sems = refs[count:]
    width = groups * HEAD_DIM
    rows = groups * steps * PER_GROUP
    tokens = bias_ref.shape[2]
    rows_kv = parts[0][...]
    if count > 1:
        total = rows_kv.astype(jnp.float32)
        for part in parts[1:]:
            total = total + part[...].astype(jnp.float32)
        rows_kv = total.astype(jnp.bfloat16)
    if rows_kv.shape[0] < tokens:
        rows_kv = jnp.concatenate(
            [rows_kv, jnp.zeros((tokens - rows_kv.shape[0], 2 * width), jnp.bfloat16)], axis=0
        )
    k, v = rows_kv[:, :width], rows_kv[:, width:]
    s = (dot_nt(q_ref[...], k) * SCALE).reshape(reqs, rows // 8, 8, tokens) + bias_ref[...][:, None]
    s = s.reshape(reqs * rows, tokens)
    m_old = m_ref[...]
    m = jnp.maximum(m_old, jnp.max(s, axis=1, keepdims=True))
    alpha = jnp.exp2(m_old - m)
    p_new = jnp.exp2(s - m[:, :1])
    l = l_ref[...] * alpha + jnp.sum(p_new, axis=1, keepdims=True)
    pv = jnp.dot(p_new.astype(jnp.bfloat16), v, preferred_element_type=jnp.float32)
    part = rows // groups
    pv = pv.reshape(reqs, groups, part, width)
    pv = jnp.stack([pv[:, g, :, g * HEAD_DIM : (g + 1) * HEAD_DIM] for g in range(groups)], axis=1)
    of[...] = (o_ref[...] * alpha + pv.reshape(reqs * rows, HEAD_DIM)) / l
    copies = []
    for r in range(reqs):
        for g in range(groups):
            for h in range(PER_GROUP):
                at = (g * PER_GROUP + h) * HEAD_DIM
                out_ref[r, :, at : at + HEAD_DIM] = of[
                    pl.ds(r * rows + g * steps * PER_GROUP + h, steps, stride=PER_GROUP), :
                ].astype(jnp.bfloat16)
        copies.append(pltpu.make_async_copy(out_ref.at[r], out_hbm.at[r], sems.at[r]))
        copies[r].start()
    for copy in copies:
        copy.wait()


def prompt(state, parts, query):
    reqs, steps = query.shape[:2]
    groups = parts[0].shape[1] // (2 * HEAD_DIM)
    q, o, m, l, bias = state
    return pl.pallas_call(
        functools.partial(prompt_kernel, reqs, steps, groups, len(parts)),
        out_shape=pltpu.HBM(query.shape, jnp.bfloat16),
        in_specs=[VMEM] * (5 + len(parts)),
        out_specs=HBM,
        scratch_shapes=[
            pltpu.VMEM(query.shape, jnp.bfloat16),
            pltpu.VMEM(o.shape, jnp.float32),
            pltpu.SemaphoreType.DMA((reqs,)),
        ],
        compiler_params=pltpu.CompilerParams(vmem_limit_bytes=24 * 2**20),
        name="prompt",
    )(*parts, q, o, m, l, bias)


def add_kernel(parts_ref, out_ref):
    total = parts_ref[0].astype(jnp.float32)
    for k in range(1, parts_ref.shape[0]):
        total = total + parts_ref[k].astype(jnp.float32)
    out_ref[...] = total.astype(jnp.bfloat16)


def add(parts):
    return pl.pallas_call(
        add_kernel,
        out_shape=jax.ShapeDtypeStruct(parts.shape[1:], jnp.bfloat16),
        in_specs=[VMEM],
        out_specs=VMEM,
        compiler_params=pltpu.CompilerParams(vmem_limit_bytes=24 * 2**20),
        name="add",
    )(parts)


def on_device(
    pool, prompt_hidden, kv_weight, cache_kv, block_table, cache_len, page_request, prompt_len, query, new_kv
):
    reqs, page, pages = query.shape[0], cache_kv.shape[2], page_request.shape[0]
    tokens = pages * page
    inputs = (block_table, cache_len, page_request, prompt_len, cache_kv, query, new_kv)
    if pool == 8 and pages <= 8:
        sizes = step_sizes(pages, reqs)
        firsts = sorted({size[0] for size in sizes})
        outs = project(prompt_hidden, kv_weight, page_request, reqs, page, sizes)
        sends, (keep, *plans, choice) = outs[: 3 * len(firsts)], outs[3 * len(firsts) :]

        def share(size, sends, keep, plans, inputs):
            def trade(x, bits):
                return lax.ppermute(x, "pool", [(i, i ^ bits) for i in range(pool)])

            at = 3 * firsts.index(size[0])
            got = [trade(sends[at + bits - 1], bits) for bits in (3, 1, 2)]
            state = cached(*inputs, HEAD_DIM, True, keep)
            send, mine = fold(keep, got, plans, size[1] * page, state[2])
            return prompt(state, [mine, trade(send, 4)], query)

        branches = [functools.partial(share, size) for size in sizes]
        choice = lax.optimization_barrier(choice.reshape(()))
        return lax.switch(choice, branches, sends, keep, plans, inputs)
    [own] = project(prompt_hidden, kv_weight, page_request, reqs, page, [])
    got = lax.all_to_all(own.reshape(pool, tokens // pool, -1), "pool", 0, 0, tiled=True)
    mine = add(got)
    shared = lax.all_to_all(jnp.broadcast_to(mine, got.shape), "pool", 0, 0, tiled=True)
    state = cached(*inputs, tokens, False, mine)
    return prompt(state, [shared.reshape(tokens, -1)], query)


def solution(mesh):
    in_specs = (
        P("pool", "groups"),
        P(None, "pool", "tp"),
        P(None, ("groups", "pool"), None, "tp"),
        P(("groups", "pool"), None),
        P(("groups", "pool")),
        P("groups"),
        P(("groups", "pool")),
        P(("groups", "pool"), None, "tp"),
        P(None, ("groups", "pool"), None, "tp"),
    )
    out_specs = P(("groups", "pool"), None, "tp")
    return jax.shard_map(
        functools.partial(on_device, mesh.shape["pool"]),
        mesh=mesh,
        in_specs=in_specs,
        out_specs=out_specs,
        check_vma=False,
    )
```

```python
import functools
import math

import jax
import jax.numpy as jnp
from jax import lax
from jax.experimental import pallas as pl
from jax.experimental.pallas import tpu as pltpu
from jax.sharding import PartitionSpec as P

HEAD_DIM = 128
PER_GROUP = 8
SCALE = HEAD_DIM**-0.5 * math.log2(math.e)
LOW = -1e30

VMEM = pl.BlockSpec(memory_space=pltpu.VMEM)
SMEM = pl.BlockSpec(memory_space=pltpu.SMEM)
HBM = pl.BlockSpec(memory_space=pltpu.HBM)
ANY = pl.BlockSpec(memory_space=pl.ANY)


def in_hbm(*arrays):
    return [pltpu.with_memory_space_constraint(x, pltpu.HBM) for x in arrays]


def dot_nt(a, b):
    return lax.dot_general(a, b, (((1,), (1,)), ((), ())), preferred_element_type=jnp.float32)


def pages_before(owner_ref, request):
    count = jnp.int32(0)
    for p in range(owner_ref.shape[0]):
        count = count + jnp.where(owner_ref[p] < request, 1, 0)
    return count


def step_sizes(page_total, reqs):
    most = (page_total - 1, min(page_total, page_total // 4 + reqs - 1))
    usual = [(3, 2), (3, 3), (4, 2), (4, 3), (5, 4)]
    return [u for u in usual if u[0] < most[0] and u[1] <= most[1]] + [most]


def plan_steps(owner_ref, reqs, page, sizes, choice_ref, lists, plan_refs):
    me = lax.axis_index("pool")
    page_total = owner_ref.shape[0]
    for ref in lists:
        for p in range(page_total):
            ref[p] = jnp.int32(0)
    filled = [jnp.int32(0)] * 6
    counts = [jnp.int32(0)] * 2
    for p in range(page_total):
        owner = lax.div(owner_ref[p], jnp.int32(reqs))
        counts[0] = counts[0] + lax.shift_left(jnp.int32(1), 4 * (owner & 3))
        counts[1] = counts[1] + lax.shift_left(jnp.int32(1), 4 * owner)
        away = owner ^ me
        place = filled[0]
        for i in range(6):
            if i < 4:
                here, value = (away & 3) == i, jnp.int32(p)
            else:
                here, value = away == 4 * (5 - i), place
            lists[i][jnp.where(here, filled[i], page_total)] = value
            filled[i] = filled[i] + jnp.where(here, 1, 0)
    most = []
    for count, classes in zip(counts, (4, 8)):
        top = jnp.int32(0)
        for c in range(classes):
            top = jnp.maximum(top, lax.shift_right_logical(count, jnp.int32(4 * c)) & 15)
        most.append(top)
    choice = jnp.int32(len(sizes) - 1)
    for i in reversed(range(len(sizes) - 1)):
        fits = (most[0] <= sizes[i][0]) & (most[1] <= sizes[i][1])
        choice = jnp.where(fits, i, choice)
    choice_ref[0] = choice
    row = lax.broadcasted_iota(jnp.int32, (page, HEAD_DIM), 0)
    for ref, plan in zip(lists[4:], plan_refs):
        for j in range(plan.shape[0] // page):
            plan[j * page : (j + 1) * page, :] = ref[j] * page + row


def project_kernel(pieces, reqs, page, sizes, hidden_ref, weight_ref, owner_hbm, *rest):
    if sizes:
        count = 3 * len({size[0] for size in sizes})
        sends, (keep_ref, *plan_refs, choice_ref) = rest[:count], rest[count : count + 4]
        own_ref, hidden_buf, turned_buf, weight_buf, owner_ref, sems, small, *lists = rest[count + 4 :]
    else:
        own_ref, hidden_buf, turned_buf, weight_buf, owner_ref, sems, small = rest
    cols = weight_ref.shape[2]
    size = hidden_ref.shape[0] // pieces
    hidden_copy = pltpu.make_async_copy(hidden_ref, hidden_buf, small.at[0])
    owner_copy = pltpu.make_async_copy(owner_hbm, owner_ref, small.at[1])
    copies = []
    for i in range(pieces):
        at = pl.ds(i * size, size)
        copies.append(
            pltpu.make_async_copy(weight_ref.at[:, at], weight_buf.at[:, at], sems.at[i])
        )
    for copy in [hidden_copy, owner_copy] + copies:
        copy.start()
    owner_copy.wait()
    if sizes:
        plan_steps(owner_ref, reqs, page, sizes, choice_ref, lists, plan_refs)
    hidden_copy.wait()
    turned_buf[...] = hidden_buf[...].T
    totals = [0.0, 0.0]
    for i in range(pieces):
        copies[i].wait()
        at = slice(i * size, (i + 1) * size)
        for kind in range(2):
            totals[kind] = totals[kind] + jnp.dot(
                turned_buf[:, at], weight_buf[kind, at], preferred_element_type=jnp.float32
            )
    for kind in range(2):
        own_ref[:, kind * cols : (kind + 1) * cols] = totals[kind].astype(jnp.bfloat16)
    if sizes:

        def pack(pages, chosen):
            for j in range(pages):
                at = slice(j * page, (j + 1) * page)
                for i, out in enumerate([keep_ref] + chosen):
                    begin = pl.multiple_of(lists[i][j] * page, page)
                    out[at, :] = own_ref[pl.ds(begin, page), :]

        firsts = [first for first, _ in sizes]
        for k, first in enumerate(sorted(set(firsts))):
            places = [i for i, other in enumerate(firsts) if other == first]
            chosen = (choice_ref[0] >= places[0]) & (choice_ref[0] <= places[-1])
            pl.when(chosen)(functools.partial(pack, first, list(sends[3 * k : 3 * k + 3])))


def project(hidden, weight, owner, reqs, page, sizes):
    tokens, cols = hidden.shape[1], weight.shape[2]
    pieces = max(1, hidden.shape[0] // 512)
    rows = lambda n: jax.ShapeDtypeStruct((n * page, 2 * cols), jnp.bfloat16)
    scratch = [
        pltpu.VMEM(hidden.shape, jnp.bfloat16),
        pltpu.VMEM(hidden.shape[::-1], jnp.bfloat16),
        pltpu.VMEM(weight.shape, jnp.bfloat16),
        pltpu.SMEM(owner.shape, jnp.int32),
        pltpu.SemaphoreType.DMA((pieces,)),
        pltpu.SemaphoreType.DMA((2,)),
    ]
    if sizes:
        first, second = sizes[-1]
        plan = jax.ShapeDtypeStruct((second * page, HEAD_DIM), jnp.int32)
        out_shape = [rows(n) for n in sorted({size[0] for size in sizes}) for _ in range(3)]
        out_shape += [rows(first), plan, plan]
        out_specs = [VMEM] * len(out_shape) + [SMEM]
        out_shape += [pltpu.SMEM((1,), jnp.int32)]
        scratch = [pltpu.VMEM((tokens, 2 * cols), jnp.bfloat16)] + scratch
        scratch += [pltpu.SMEM((owner.shape[0] + 1,), jnp.int32)] * 6
    else:
        out_shape, out_specs = [rows(tokens // page)], [VMEM]
    return pl.pallas_call(
        functools.partial(project_kernel, pieces, reqs, page, sizes),
        out_shape=out_shape,
        in_specs=[HBM] * 3,
        out_specs=out_specs,
        scratch_shapes=scratch,
        compiler_params=pltpu.CompilerParams(vmem_limit_bytes=24 * 2**20),
        cost_estimate=pl.CostEstimate(
            flops=4 * hidden.size * cols,
            bytes_accessed=2 * (hidden.size + weight.size + tokens * 2 * cols),
            transcendentals=0,
        ),
        name="project",
    )(*in_hbm(hidden, weight, owner))


def fold_kernel(keep_ref, *refs):
    got, (send_plan, keep_plan, _, send_out, keep_out) = refs[:-5], refs[-5:]
    rows = got[0].shape[0]
    total = keep_ref[:rows].astype(jnp.float32)
    for ref in got:
        total = total + ref[...].astype(jnp.float32)
    pad = jnp.zeros((HEAD_DIM - rows, total.shape[1]), jnp.bfloat16)
    total = jnp.concatenate([total.astype(jnp.bfloat16), pad], axis=0)
    for plan, out in ((send_plan, send_out), (keep_plan, keep_out)):
        at = plan[: out.shape[0]]
        col = lax.broadcasted_iota(jnp.int32, at.shape, 1)
        take = jnp.where(at == col, 1.0, 0.0).astype(jnp.bfloat16)
        out[...] = jnp.dot(take, total, preferred_element_type=jnp.float32).astype(jnp.bfloat16)


def fold(keep, got, plans, rows, after):
    out = jax.ShapeDtypeStruct((rows, keep.shape[1]), jnp.bfloat16)
    return pl.pallas_call(
        fold_kernel,
        out_shape=[out, out],
        in_specs=[VMEM] * (3 + len(got)) + [ANY],
        out_specs=[VMEM] * 2,
        compiler_params=pltpu.CompilerParams(vmem_limit_bytes=24 * 2**20),
        cost_estimate=pl.CostEstimate(
            flops=4 * rows * keep.size, bytes_accessed=8 * keep.size, transcendentals=0
        ),
        name="fold",
    )(keep, *got, *plans, after)


def cached_kernel(
    reqs, steps, groups, pages, packed,
    table_hbm, len_hbm, owner_hbm, prompt_hbm, cache_ref, query_hbm, new_hbm, after_ref,
    q_out, o_out, m_out, l_out, bias_out,
    table_ref, len_ref, owner_ref, prompt_ref, query_ref, new_ref, kbuf, vbuf, qf, newf, sems, small,
):
    page = kbuf.shape[1]
    span = pages * page
    rows = groups * steps * PER_GROUP
    pieces = sems.shape[1]
    size = kbuf.shape[0] // pieces
    first_loads = [
        pltpu.make_async_copy(src, dst, small.at[i])
        for i, (src, dst) in enumerate(
            (
                (query_hbm, query_ref),
                (new_hbm, new_ref),
                (table_hbm, table_ref),
                (len_hbm, len_ref),
                (owner_hbm, owner_ref),
                (prompt_hbm, prompt_ref),
            )
        )
    ]
    copies = [
        [
            pltpu.make_async_copy(
                cache_ref.at[kind, pl.ds(i * size, size)],
                buf.at[pl.ds(i * size, size)],
                sems.at[kind, i],
            )
            for i in range(pieces)
        ]
        for kind, buf in enumerate((kbuf, vbuf))
    ]
    for copy in first_loads + copies[0] + copies[1]:
        copy.start()
    for copy in first_loads:
        copy.wait()

    me = lax.axis_index("pool")
    firsts = [pages_before(owner_ref, me * reqs + r) for r in range(reqs + 1)]
    begin = firsts[0] * page if packed else 0
    col = lax.broadcasted_iota(jnp.int32, bias_out.shape[1:], 1) + begin
    for r, (first, last) in enumerate(zip(firsts, firsts[1:])):
        end = jnp.minimum(first * page + prompt_ref[r], last * page)
        bias_out[r] = jnp.where((col >= first * page) & (col < end), 0.0, LOW)

    for r in range(reqs):
        for g in range(groups):
            for h in range(PER_GROUP):
                at = (g * PER_GROUP + h) * HEAD_DIM
                qf[pl.ds(r * rows + g * steps * PER_GROUP + h, steps, stride=PER_GROUP), :] = query_ref[
                    r, :, at : at + HEAD_DIM
                ].astype(jnp.float32)
    q_all = qf[...]
    row = lax.broadcasted_iota(jnp.int32, q_all.shape, 0)
    row_group = (row // (steps * PER_GROUP)) % groups
    q_out[...] = jnp.concatenate(
        [jnp.where(row_group == g, q_all, 0.0).astype(jnp.bfloat16) for g in range(groups)], axis=1
    )

    slot = HEAD_DIM // reqs
    newf[...] = jnp.zeros_like(newf)
    for kind in range(2):
        for r in range(reqs):
            newf[kind, r * slot : r * slot + steps, :] = new_ref[kind, r].astype(jnp.float32)
    new_k = newf[0].astype(jnp.bfloat16)
    new_v = newf[1].astype(jnp.bfloat16)

    for copy in copies[0]:
        copy.wait()
    scores, news, maxes = [], [], []
    for r in range(reqs):
        q = q_out[r * rows : (r + 1) * rows, :]
        s_new = dot_nt(q, new_k) * SCALE
        row = lax.broadcasted_iota(jnp.int32, s_new.shape, 0)
        col = lax.broadcasted_iota(jnp.int32, s_new.shape, 1) - r * slot
        step = (row // PER_GROUP) % steps
        s_new = jnp.where((col >= 0) & (col <= step), s_new, LOW)
        news.append(s_new)
        k = jnp.concatenate([kbuf[table_ref[r, j]] for j in range(pages)], axis=0)
        s = dot_nt(q, k) * SCALE
        col = lax.broadcasted_iota(jnp.int32, s.shape, 1)
        s = jnp.where(col < len_ref[r], s, LOW)
        scores.append(s)
        top = s_new
        for c in range(span // HEAD_DIM):
            top = jnp.maximum(top, s[:, c * HEAD_DIM : (c + 1) * HEAD_DIM])
        m = jnp.max(top, axis=1, keepdims=True)
        maxes.append(m)
        m_out[r * rows : (r + 1) * rows, :] = jnp.broadcast_to(m, (rows, HEAD_DIM))
    for copy in copies[1]:
        copy.wait()
    for r in range(reqs):
        p = jnp.exp2(scores[r] - maxes[r])
        p_new = jnp.exp2(news[r] - maxes[r])
        total = p_new
        for c in range(span // HEAD_DIM):
            total = total + p[:, c * HEAD_DIM : (c + 1) * HEAD_DIM]
        l_out[r * rows : (r + 1) * rows, :] = jnp.broadcast_to(
            jnp.sum(total, axis=1, keepdims=True), (rows, HEAD_DIM)
        )
        v = jnp.concatenate([vbuf[table_ref[r, j]] for j in range(pages)], axis=0)
        o = jnp.dot(p.astype(jnp.bfloat16), v, preferred_element_type=jnp.float32)
        o = o + jnp.dot(p_new.astype(jnp.bfloat16), new_v, preferred_element_type=jnp.float32)
        part = rows // groups
        for g in range(groups):
            o_out[r * rows + g * part : r * rows + (g + 1) * part, :] = o[
                g * part : (g + 1) * part, g * HEAD_DIM : (g + 1) * HEAD_DIM
            ]


def cached(table, length, owner, prompt_len, cache, query, new, tokens, packed, after):
    reqs, steps = query.shape[:2]
    groups = cache.shape[3] // HEAD_DIM
    pages, page = table.shape[1], cache.shape[2]
    rows = reqs * groups * steps * PER_GROUP
    flat = jax.ShapeDtypeStruct((rows, HEAD_DIM), jnp.float32)
    return pl.pallas_call(
        functools.partial(cached_kernel, reqs, steps, groups, pages, packed),
        out_shape=[
            jax.ShapeDtypeStruct((rows, groups * HEAD_DIM), jnp.bfloat16),
            flat,
            flat,
            flat,
            jax.ShapeDtypeStruct((reqs, 8, tokens), jnp.float32),
        ],
        in_specs=[HBM] * 7 + [ANY],
        out_specs=[VMEM] * 5,
        scratch_shapes=[
            pltpu.SMEM(table.shape, jnp.int32),
            pltpu.SMEM(length.shape, jnp.int32),
            pltpu.SMEM(owner.shape, jnp.int32),
            pltpu.SMEM(prompt_len.shape, jnp.int32),
            pltpu.VMEM(query.shape, jnp.bfloat16),
            pltpu.VMEM(new.shape, jnp.bfloat16),
            pltpu.VMEM(cache.shape[1:], jnp.bfloat16),
            pltpu.VMEM(cache.shape[1:], jnp.bfloat16),
            pltpu.VMEM((rows, HEAD_DIM), jnp.float32),
            pltpu.VMEM((2, HEAD_DIM, groups * HEAD_DIM), jnp.float32),
            pltpu.SemaphoreType.DMA((2, 4)),
            pltpu.SemaphoreType.DMA((6,)),
        ],
        compiler_params=pltpu.CompilerParams(vmem_limit_bytes=32 * 2**20),
        cost_estimate=pl.CostEstimate(
            flops=8 * rows * pages * page * HEAD_DIM,
            bytes_accessed=2 * cache.size,
            transcendentals=rows * pages * page,
        ),
        name="cached",
    )(*in_hbm(table, length, owner, prompt_len, cache, query, new), after)


def prompt_kernel(reqs, steps, groups, count, *refs):
    parts = refs[:count]
    q_ref, o_ref, m_ref, l_ref, bias_ref, out_hbm, out_ref, of, sems = refs[count:]
    width = groups * HEAD_DIM
    rows = groups * steps * PER_GROUP
    tokens = bias_ref.shape[2]
    rows_kv = parts[0][...]
    if count > 1:
        total = rows_kv.astype(jnp.float32)
        for part in parts[1:]:
            total = total + part[...].astype(jnp.float32)
        rows_kv = total.astype(jnp.bfloat16)
    if rows_kv.shape[0] < tokens:
        rows_kv = jnp.concatenate(
            [rows_kv, jnp.zeros((tokens - rows_kv.shape[0], 2 * width), jnp.bfloat16)], axis=0
        )
    k, v = rows_kv[:, :width], rows_kv[:, width:]
    part = rows // groups

    def of_group(x, g):
        return x.reshape(reqs, groups, part, x.shape[1])[:, g].reshape(reqs * part, x.shape[1])

    for g in range(groups):
        at = slice(g * HEAD_DIM, (g + 1) * HEAD_DIM)
        s = dot_nt(of_group(q_ref[:, at], g), k[:, at]) * SCALE
        s = s.reshape(reqs, part // 8, 8, tokens) + bias_ref[...][:, None]
        s = s.reshape(reqs * part, tokens)
        m_old = of_group(m_ref[...], g)
        m = jnp.maximum(m_old, jnp.max(s, axis=1, keepdims=True))
        alpha = jnp.exp2(m_old - m)
        p_new = jnp.exp2(s - m[:, :1])
        l = of_group(l_ref[...], g) * alpha + jnp.sum(p_new, axis=1, keepdims=True)
        pv = jnp.dot(p_new.astype(jnp.bfloat16), v[:, at], preferred_element_type=jnp.float32)
        out = (of_group(o_ref[...], g) * alpha + pv) / l
        for r in range(reqs):
            of[r * rows + g * part : r * rows + (g + 1) * part, :] = out[r * part : (r + 1) * part]
    copies = []
    for r in range(reqs):
        for g in range(groups):
            for h in range(PER_GROUP):
                at = (g * PER_GROUP + h) * HEAD_DIM
                out_ref[r, :, at : at + HEAD_DIM] = of[
                    pl.ds(r * rows + g * steps * PER_GROUP + h, steps, stride=PER_GROUP), :
                ].astype(jnp.bfloat16)
        copies.append(pltpu.make_async_copy(out_ref.at[r], out_hbm.at[r], sems.at[r]))
        copies[r].start()
    for copy in copies:
        copy.wait()


def prompt(state, parts, query):
    reqs, steps = query.shape[:2]
    groups = parts[0].shape[1] // (2 * HEAD_DIM)
    q, o, m, l, bias = state
    return pl.pallas_call(
        functools.partial(prompt_kernel, reqs, steps, groups, len(parts)),
        out_shape=pltpu.HBM(query.shape, jnp.bfloat16),
        in_specs=[VMEM] * (5 + len(parts)),
        out_specs=HBM,
        scratch_shapes=[
            pltpu.VMEM(query.shape, jnp.bfloat16),
            pltpu.VMEM(o.shape, jnp.float32),
            pltpu.SemaphoreType.DMA((reqs,)),
        ],
        compiler_params=pltpu.CompilerParams(vmem_limit_bytes=24 * 2**20),
        name="prompt",
    )(*parts, q, o, m, l, bias)


def add_kernel(parts_ref, out_ref):
    total = parts_ref[0].astype(jnp.float32)
    for k in range(1, parts_ref.shape[0]):
        total = total + parts_ref[k].astype(jnp.float32)
    out_ref[...] = total.astype(jnp.bfloat16)


def add(parts):
    return pl.pallas_call(
        add_kernel,
        out_shape=jax.ShapeDtypeStruct(parts.shape[1:], jnp.bfloat16),
        in_specs=[VMEM],
        out_specs=VMEM,
        compiler_params=pltpu.CompilerParams(vmem_limit_bytes=24 * 2**20),
        name="add",
    )(parts)


def on_device(
    pool, prompt_hidden, kv_weight, cache_kv, block_table, cache_len, page_request, prompt_len, query, new_kv
):
    reqs, page, pages = query.shape[0], cache_kv.shape[2], page_request.shape[0]
    tokens = pages * page
    inputs = (block_table, cache_len, page_request, prompt_len, cache_kv, query, new_kv)
    if pool == 8 and pages <= 8:
        sizes = step_sizes(pages, reqs)
        firsts = sorted({size[0] for size in sizes})
        outs = project(prompt_hidden, kv_weight, page_request, reqs, page, sizes)
        sends, (keep, *plans, choice) = outs[: 3 * len(firsts)], outs[3 * len(firsts) :]

        def share(size, sends, keep, plans, inputs):
            def trade(x, bits):
                return lax.ppermute(x, "pool", [(i, i ^ bits) for i in range(pool)])

            at = 3 * firsts.index(size[0])
            got = [trade(sends[at + bits - 1], bits) for bits in (3, 1, 2)]
            state = cached(*inputs, HEAD_DIM, True, keep)
            send, mine = fold(keep, got, plans, size[1] * page, state[2])
            return prompt(state, [mine, trade(send, 4)], query)

        branches = [functools.partial(share, size) for size in sizes]
        choice = lax.optimization_barrier(choice.reshape(()))
        return lax.switch(choice, branches, sends, keep, plans, inputs)
    [own] = project(prompt_hidden, kv_weight, page_request, reqs, page, [])
    got = lax.all_to_all(own.reshape(pool, tokens // pool, -1), "pool", 0, 0, tiled=True)
    mine = add(got)
    shared = lax.all_to_all(jnp.broadcast_to(mine, got.shape), "pool", 0, 0, tiled=True)
    state = cached(*inputs, tokens, False, mine)
    return prompt(state, [shared.reshape(tokens, -1)], query)


def solution(mesh):
    in_specs = (
        P("pool", "groups"),
        P(None, "pool", "tp"),
        P(None, ("groups", "pool"), None, "tp"),
        P(("groups", "pool"), None),
        P(("groups", "pool")),
        P("groups"),
        P(("groups", "pool")),
        P(("groups", "pool"), None, "tp"),
        P(None, ("groups", "pool"), None, "tp"),
    )
    out_specs = P(("groups", "pool"), None, "tp")
    return jax.shard_map(
        functools.partial(on_device, mesh.shape["pool"]),
        mesh=mesh,
        in_specs=in_specs,
        out_specs=out_specs,
        check_vma=False,
    )
```
